32 devices in a mesh: groups: 2 (over x), pose: 16 (over z, y, core).
Axes of the slice: x: 2, y: 2, z: 4, core: 2. Of those that a mesh axis runs over, the one named last changes fastest.
Arguments:
- images: bfloat16 [32, 36864], P(('groups', 'pose')), parts along dimension 0
- ctf_class: int32 [32], P(('groups', 'pose')), parts along dimension 0, may hold values from 0 to 15
- projections: bfloat16 [2048, 36864], P(('groups', 'pose')), parts along dimension 0
- ctf_table: float32 [16, 18432], replicated, may hold values from 0.1 to 1
- tile_mask: int32 [2, 128], P('groups', 'pose'), parts along dimension 0, may hold values from 0 to 1, as said below
Outputs:
- back_sums: bfloat16 [2048, 36864], P(('groups', 'pose')), parts along dimension 0
- pose_totals: float32 [2048], P(('groups', 'pose')), parts along dimension 0
The draws below stay inside these ranges and needn't reach their ends.
There are 2 independent parts, one for each index of `groups`. The reference program is written for one: setup_inputs(seed, part) draws one part's arguments, and reference() takes and returns one part's arrays. A program takes and returns all parts, laid end to end along the dimension named above; an argument that names none is the same for every part. Nothing has to cross between parts.
Inputs may be any that keep to these rules, and one draw needn't show every extreme that they name: `tile_mask`: every block of 16 images has at least one significant tile of 8 poses.
All inputs are finite; a program needn't handle non-finite values.
Results may differ from the reference program's by a relative error of at most 0.0077.
Values may be sent and summed in bfloat16 or wider, within the bound.
A program may use at most 128 MiB of HBM per device.

```python
import math
import jax
import jax.numpy as jnp
from jax import lax

BOX = 192
P_SIZE = 36864
NCTF = 16
NSHIFT = 5
IMG_TILE = 16
POSE_TILE = 8
NIMG = 16
NPOSE = 1024


def reference_row(key, pose_index):
    row_key = jax.random.fold_in(jax.random.fold_in(key, 2), pose_index)
    return jax.random.normal(row_key, (P_SIZE,), jnp.float32) * (3.0 / math.sqrt(P_SIZE))


def forced_tiles(key):
    return jax.random.randint(jax.random.fold_in(key, 7), (NIMG // IMG_TILE,), 0, NPOSE // POSE_TILE)


def draw_projections(key, part):
    pose_index = jnp.arange(NPOSE, dtype=jnp.int32)
    return jax.vmap(lambda index_value: reference_row(key, index_value))(pose_index).astype(jnp.bfloat16)


def draw_tile_mask(key, part):
    forced = forced_tiles(key)
    tile_count = NPOSE // POSE_TILE
    levels = jax.random.randint(jax.random.fold_in(key, 8), (tile_count,), 1, 7)
    rolls = jax.random.randint(jax.random.fold_in(key, 9), (NIMG // IMG_TILE, tile_count), 0, 8)
    columns = jnp.arange(tile_count, dtype=jnp.int32)
    chosen = (rolls < levels[None, :]) | (columns[None, :] == forced[:, None])
    return chosen.astype(jnp.int32)


def draw_images(key, part):
    noise = jax.random.normal(jax.random.fold_in(key, 1), (NIMG, P_SIZE), jnp.float32)
    return noise.astype(jnp.bfloat16)


def place_ends(entries, stream_key, least, top_value):
    index_at = [jax.random.randint(jax.random.fold_in(stream_key, axis), (), 0, length) for axis, length in enumerate(entries.shape)]
    longest = entries.shape.index(max(entries.shape))
    neighbour = index_at[:longest] + [(index_at[longest] + 1) % entries.shape[longest]] + index_at[longest + 1:]
    return entries.at[tuple(index_at)].set(least).at[tuple(neighbour)].set(top_value)


def setup_inputs(seed: int = 0, part: int = 0) -> dict:
    keys = jax.random.split(jax.random.key(seed), 6)
    part_splits = jax.random.split(jax.random.fold_in(keys[5], part), 6)
    images = draw_images(jax.random.fold_in(jax.random.fold_in(keys[5], part), 71), part)
    ctf_class = place_ends(jax.random.randint(part_splits[1], (NIMG,), 0, NCTF), jax.random.fold_in(part_splits[1], 1), 0, NCTF - 1).astype(jnp.int32)
    projections = draw_projections(jax.random.fold_in(jax.random.fold_in(keys[5], part), 71), part)
    ctf_table = jnp.clip(jax.random.uniform(keys[3], (NCTF, P_SIZE // 2), jnp.float32, 0.1, 1.0), 0.1, 1.0)
    tile_mask = draw_tile_mask(jax.random.fold_in(jax.random.fold_in(keys[5], part), 71), part)
    return dict(images=images, ctf_class=ctf_class, projections=projections, ctf_table=ctf_table, tile_mask=tile_mask)


shift_rows = (0.0, 1.0, -1.0, 0.0, 0.0)
shift_cols = (0.0, 0.0, 0.0, 1.0, -1.0)
floor_score = -1.0e30


def phase_tables(box_size):
    half_box = box_size // 2
    coeff_index = jnp.arange(box_size * half_box, dtype=jnp.int32)
    row_index = coeff_index // half_box
    col_index = coeff_index % half_box
    freq_x = jnp.where(row_index < half_box, row_index, row_index - box_size).astype(jnp.float32)
    freq_y = col_index.astype(jnp.float32)
    step_x = jnp.array(shift_rows, jnp.float32)[:, None]
    step_y = jnp.array(shift_cols, jnp.float32)[:, None]
    phases = (2.0 * math.pi / box_size) * (step_x * freq_x[None, :] + step_y * freq_y[None, :])
    return jnp.cos(phases), jnp.sin(phases)


def class_rows(classes, ctf_count):
    return (classes[:, None] == jnp.arange(ctf_count, dtype=jnp.int32)[None, :]).astype(jnp.float32)


def make_shifted(pixels, classes, ctf_table, cosine_tab, sine_table):
    half_len = pixels.shape[1] // 2
    one_hot = class_rows(classes, ctf_table.shape[0])
    factor = jnp.dot(one_hot, ctf_table, precision=lax.Precision.HIGHEST)[:, None, :]
    real_part = pixels[:, :half_len].astype(jnp.float32)[:, None, :]
    imag_part = pixels[:, half_len:].astype(jnp.float32)[:, None, :]
    shifted_re = (real_part * cosine_tab[None] + imag_part * sine_table[None]) * factor
    shifted_im = (imag_part * cosine_tab[None] - real_part * sine_table[None]) * factor
    return jnp.concatenate([shifted_re, shifted_im], axis=2).astype(jnp.bfloat16)


def norm_terms(projections, ctf_table):
    squared = ctf_table * ctf_table
    squared = jnp.concatenate([squared, squared], axis=1)
    proj_f = projections.astype(jnp.float32)
    return jnp.dot(squared, (proj_f * proj_f).T, precision=lax.Precision.HIGHEST)


def reference(images, ctf_class, projections, ctf_table, tile_mask):
    cosine_tab, sine_table = phase_tables(BOX)
    stacked = make_shifted(images, ctf_class, ctf_table, cosine_tab, sine_table).reshape(NIMG * NSHIFT, P_SIZE)
    norm_table = norm_terms(projections, ctf_table)
    penalty = jnp.dot(class_rows(ctf_class, NCTF), norm_table, precision=lax.Precision.HIGHEST)
    raw_scores = jnp.dot(stacked, projections.T, preferred_element_type=jnp.float32).reshape(NIMG, NSHIFT, NPOSE)
    scores = raw_scores - 0.5 * penalty[:, None, :]
    allowed = jnp.repeat(jnp.repeat(tile_mask, IMG_TILE, axis=0), POSE_TILE, axis=1) > 0
    masked = jnp.where(allowed[:, None, :], scores, floor_score)
    peak = jnp.max(masked, axis=(1, 2))
    exponent = jnp.where(allowed[:, None, :], jnp.exp(masked - peak[:, None, None]), 0.0)
    denominator = jnp.sum(exponent, axis=(1, 2))
    weights = (exponent / denominator[:, None, None]).astype(jnp.bfloat16)
    rescale = NSHIFT * NPOSE / NIMG
    accumulated = lax.dot_general(weights.reshape(NIMG * NSHIFT, NPOSE), stacked, (((0,), (0,)), ((), ())), preferred_element_type=jnp.float32)
    back_sums = (rescale * accumulated).astype(jnp.bfloat16)
    pose_totals = rescale * jnp.sum(weights.astype(jnp.float32), axis=(0, 1))
    return back_sums, pose_totals
```

```python
import functools
import math

import jax
import jax.numpy as jnp
import numpy as np
from jax import lax
from jax.experimental import pallas as pl
from jax.experimental.pallas import tpu as pltpu
from jax.sharding import PartitionSpec as P

BOX = 192
IMG_TILE = 16
POSE_TILE = 8


shift_rows = (0.0, 1.0, -1.0, 0.0, 0.0)
shift_cols = (0.0, 0.0, 0.0, 1.0, -1.0)
floor_score = -1e30


def joined(value, axis, join):
    pieces = jax.tree.map(lambda part: lax.all_gather(part, axis), value)
    head = jax.tree.map(lambda part: part[0], pieces)
    tail = jax.tree.map(lambda part: part[1:], pieces)
    running, _ = lax.scan(lambda running, slab: (join(running, slab), None), head, tail)
    return running


def phase_tables(box_size):
    half_box = box_size // 2
    coeff_index = jnp.arange(box_size * half_box, dtype=jnp.int32)
    row_index = coeff_index // half_box
    col_index = coeff_index % half_box
    freq_x = jnp.where(row_index < half_box, row_index, row_index - box_size).astype(jnp.float32)
    freq_y = col_index.astype(jnp.float32)
    step_x = jnp.array(shift_rows, jnp.float32)[:, None]
    step_y = jnp.array(shift_cols, jnp.float32)[:, None]
    phases = 2.0 * math.pi / box_size * (step_x * freq_x[None, :] + step_y * freq_y[None, :])
    return (jnp.cos(phases), jnp.sin(phases))


def class_rows(classes, ctf_count):
    return (classes[:, None] == jnp.arange(ctf_count, dtype=jnp.int32)[None, :]).astype(jnp.float32)


def make_shifted(pixels, classes, ctf_table, cosine_tab, sine_table):
    half_len = pixels.shape[1] // 2
    one_hot = class_rows(classes, ctf_table.shape[0])
    factor = jnp.dot(one_hot, ctf_table, precision=lax.Precision.HIGHEST)[:, None, :]
    real_part = pixels[:, :half_len].astype(jnp.float32)[:, None, :]
    imag_part = pixels[:, half_len:].astype(jnp.float32)[:, None, :]
    shifted_re = (real_part * cosine_tab[None] + imag_part * sine_table[None]) * factor
    shifted_im = (imag_part * cosine_tab[None] - real_part * sine_table[None]) * factor
    return jnp.concatenate([shifted_re, shifted_im], axis=2).astype(jnp.bfloat16)


def norm_terms(projections, ctf_table):
    squared = ctf_table * ctf_table
    squared = jnp.concatenate([squared, squared], axis=1)
    proj_f = projections.astype(jnp.float32)
    return jnp.dot(squared, (proj_f * proj_f).T, precision=lax.Precision.HIGHEST)


def combine_stats(earlier, latter):
    highest = jnp.maximum(earlier[0], latter[0])
    return (
        highest,
        earlier[1] * jnp.exp(earlier[0] - highest) + latter[1] * jnp.exp(latter[0] - highest),
    )


LANES = 128
CHUNK = 1024
NT = (((1,), (1,)), ((), ()))


def phase_rows(box_size):
    half_box = box_size // 2
    coeff_index = np.arange(box_size * half_box)
    row_index = coeff_index // half_box
    freq_x = np.where(row_index < half_box, row_index, row_index - box_size)
    freq_y = coeff_index % half_box
    turn = 2.0 * math.pi / box_size
    rows = [np.cos(turn * freq_x), np.sin(turn * freq_x), np.cos(turn * freq_y), np.sin(turn * freq_y)]
    return np.stack(rows + rows).astype(np.float32)


def split_bf16(value, pieces):
    parts = []
    for _ in range(pieces):
        part = value.astype(jnp.bfloat16)
        parts.append(part)
        value = value - part.astype(jnp.float32)
    return jnp.concatenate(parts, axis=0)


def posterior_kernel(
    n, factors, rescale, cls_ref, mask_ref, img_hbm, proj_hbm, ctf_hbm, tab_hbm,
    weights_ref, totals_ref, shifted_hbm,
    slots, imgf, proj, ctf, tab, shifted, stats,
    load_sem, img_sem, send_sem, recv_sem, stat_send, stat_recv, out_sem,
):
    nz, ny, nc = factors
    me = lax.axis_index("pose")
    core = lax.rem(me, nc)
    row = lax.rem(lax.div(me, nc), ny)
    deep = lax.div(me, nc * ny)

    def device(z, y, c):
        return (z * ny + y) * nc + c

    poses, width = proj.shape
    half = width // 2
    quarter = half // 2
    img_rows = width // LANES
    slot_rows = slots.shape[1]
    ctf_count = ctf.shape[0]

    loads = [
        pltpu.make_async_copy(ctf_hbm, ctf, load_sem.at[0]),
        pltpu.make_async_copy(tab_hbm, tab, load_sem.at[1]),
    ]
    for j in range(4):
        cols = pl.ds(((j % 2) * 2 + j // 2) * quarter, quarter)
        loads.append(
            pltpu.make_async_copy(proj_hbm.at[:, cols], proj.at[:, cols], load_sem.at[2 + j])
        )
    own = pltpu.make_async_copy(img_hbm, slots.at[me, pl.ds(0, img_rows)], img_sem)
    own.start()
    for copy in (loads[0], loads[2], loads[3], loads[4], loads[5], loads[1]):
        copy.start()
    barrier = pltpu.get_barrier_semaphore()
    for d in range(1, n):
        pl.semaphore_signal(
            barrier, inc=1, device_id={"pose": lax.rem(me + d, n)},
            device_id_type=pl.DeviceIdType.MESH,
        )
    label = cls_ref[0].astype(jnp.float32)
    slots[me, pl.ds(img_rows, slot_rows - img_rows), :] = jnp.full(
        (slot_rows - img_rows, LANES), label, jnp.float32
    ).astype(jnp.bfloat16)
    own.wait()
    pl.semaphore_wait(barrier, n - 1)

    started = []

    def image_copy(owner, target, slot):
        return pltpu.make_async_remote_copy(
            src_ref=slots.at[owner], dst_ref=slots.at[owner],
            send_sem=send_sem.at[slot], recv_sem=recv_sem.at[owner],
            device_id={"pose": target}, device_id_type=pl.DeviceIdType.MESH,
        )

    def send(owner, target):
        copy = image_copy(owner, target, len(started))
        copy.start()
        started.append(copy)

    def arrive(owner):
        image_copy(owner, me, 0).wait_recv()

    across = device(deep, lax.rem(row + 1, ny), core)
    beside = device(deep, row, lax.rem(core + 1, nc))
    for d in range(1, nz):
        send(me, device(lax.rem(deep + d, nz), row, core))
    send(me, across)
    send(me, beside)

    def norm_step(j, total):
        start = pl.multiple_of(j * CHUNK, CHUNK)
        real = proj[:, pl.ds(start, CHUNK)].astype(jnp.float32)
        imag = proj[:, pl.ds(pl.multiple_of(start + half, CHUNK), CHUNK)].astype(jnp.float32)
        gain = ctf[:, pl.ds(start, CHUNK)]
        power = split_bf16(real * real + imag * imag, 2)
        return total + lax.dot_general(
            split_bf16(gain * gain, 2), power, NT, preferred_element_type=jnp.float32
        )

    steps = half // CHUNK
    loads[0].wait()
    loads[2].wait()
    loads[3].wait()
    norm = lax.fori_loop(
        0, quarter // CHUNK, norm_step, jnp.zeros((2 * ctf_count, 2 * poses), jnp.float32)
    )
    for d in range(1, nz):
        owner = device(lax.rem(deep - d + nz, nz), row, core)
        arrive(owner)
        send(owner, across)
        send(owner, beside)
    loads[4].wait()
    loads[5].wait()
    norm = lax.fori_loop(quarter // CHUNK, steps, norm_step, norm)
    for d in range(nz):
        owner = device(lax.rem(deep - d + nz, nz), lax.rem(row + 1, ny), core)
        arrive(owner)
        send(owner, beside)
    norm = norm[:ctf_count] + norm[ctf_count:]
    norm = norm[:, :poses] + norm[:, poses:]
    loads[1].wait()
    for y in range(ny):
        for z in range(nz):
            arrive(device(z, y, lax.rem(core + 1, nc)))

    def widen(i, carry):
        imgf[pl.ds(pl.multiple_of(i * slot_rows, 16), slot_rows), :] = slots[i].astype(jnp.float32)
        return carry

    lax.fori_loop(0, n, widen, 0)
    labels = imgf[pl.ds(img_rows, n, stride=slot_rows), :]
    lanes = lax.broadcasted_iota(jnp.int32, (n, LANES), 1)
    one_hot = (labels == lax.rem(lanes, ctf_count).astype(jnp.float32)).astype(jnp.float32)
    picker = one_hot[:, : 3 * ctf_count].astype(jnp.bfloat16)
    half_rows = half // LANES

    def shift_step(j, total):
        start = pl.multiple_of(j * CHUNK, CHUNK)
        later = pl.multiple_of(start + half, CHUNK)
        gain = jnp.dot(
            picker, split_bf16(ctf[:, pl.ds(start, CHUNK)], 3), preferred_element_type=jnp.float32
        )
        for k in range(CHUNK // LANES):
            at = j * (CHUNK // LANES) + k
            cols = slice(k * LANES, (k + 1) * LANES)
            place = pl.ds(pl.multiple_of(start + k * LANES, LANES), LANES)
            place_im = pl.ds(pl.multiple_of(later + k * LANES, LANES), LANES)
            factor = gain[:, cols]
            real = imgf[pl.ds(at, n, stride=slot_rows), :] * factor
            imag = imgf[pl.ds(at + half_rows, n, stride=slot_rows), :] * factor
            shifted[0:n, place] = real.astype(jnp.bfloat16)
            shifted[0:n, place_im] = imag.astype(jnp.bfloat16)
            for axis in range(2):
                cosine = tab[2 * axis : 2 * axis + 1, place]
                sine = tab[2 * axis + 1 : 2 * axis + 2, place]
                first, second = real * cosine, imag * sine
                third, fourth = imag * cosine, real * sine
                low = (2 * axis + 1) * n
                shifted[low : low + n, place] = (first + second).astype(jnp.bfloat16)
                shifted[low : low + n, place_im] = (third - fourth).astype(jnp.bfloat16)
                shifted[low + n : low + 2 * n, place] = (first - second).astype(jnp.bfloat16)
                shifted[low + n : low + 2 * n, place_im] = (third + fourth).astype(jnp.bfloat16)
        for begin in (start, later):
            total = total + lax.dot_general(
                shifted[:, pl.ds(begin, CHUNK)], proj[:, pl.ds(begin, CHUNK)], NT,
                preferred_element_type=jnp.float32,
            )
        return total

    shift_count = shifted.shape[0] // n
    raw = lax.fori_loop(0, steps, shift_step, jnp.zeros((shift_count * n, poses), jnp.float32))
    written = pltpu.make_async_copy(shifted, shifted_hbm, out_sem)
    written.start()

    penalty = 0.5 * jnp.dot(
        one_hot[:, :ctf_count], norm,
        precision=lax.Precision.HIGHEST, preferred_element_type=jnp.float32,
    )
    tile = lax.div(lax.broadcasted_iota(jnp.int32, (n, poses), 1), POSE_TILE)
    allowed = jnp.zeros((n, poses), jnp.int32)
    for j in range(poses // POSE_TILE):
        allowed = jnp.where(tile == j, mask_ref[0, j], allowed)
    allowed = allowed > 0
    masked = [
        jnp.where(allowed, raw[t * n : (t + 1) * n] - penalty, floor_score)
        for t in range(shift_count)
    ]
    highest = functools.reduce(jnp.maximum, masked)
    peak = jnp.max(highest, axis=1, keepdims=True)
    mass = sum(jnp.where(allowed, jnp.exp(part - peak), 0.0) for part in masked)
    mass = jnp.sum(mass, axis=1, keepdims=True)
    stats[me, 0:n, :] = jnp.broadcast_to(peak, (n, LANES))
    stats[me, n : 2 * n, :] = jnp.broadcast_to(mass, (n, LANES))

    def stat_copy(owner, target, slot):
        return pltpu.make_async_remote_copy(
            src_ref=stats.at[owner], dst_ref=stats.at[owner],
            send_sem=stat_send.at[slot], recv_sem=stat_recv.at[owner],
            device_id={"pose": target}, device_id_type=pl.DeviceIdType.MESH,
        )

    sent = [stat_copy(me, lax.rem(me + d, n), d - 1) for d in range(1, n)]
    for copy in sent:
        copy.start()
    for d in range(1, n):
        stat_copy(lax.rem(me + d, n), me, d - 1).wait_recv()
    top = functools.reduce(jnp.maximum, [stats[j, 0:n, :] for j in range(n)])
    total = sum(stats[j, n : 2 * n, :] * jnp.exp(stats[j, 0:n, :] - top) for j in range(n))
    top = top[:, :poses]
    total = total[:, :poses]
    column = jnp.zeros((n, poses), jnp.float32)
    for t in range(shift_count):
        weight = jnp.where(allowed, jnp.exp(masked[t] - top), 0.0) / total
        weight = weight.astype(jnp.bfloat16)
        weights_ref[t * n : (t + 1) * n, :] = weight
        column = column + weight.astype(jnp.float32)
    totals_ref[...] = rescale * jnp.sum(column, axis=0, keepdims=True)
    for copy in started + sent:
        copy.wait_send()
    written.wait()


def fused(images, ctf_class, projections, ctf_table, tile_mask, n):
    poses, width = projections.shape
    shift_count = len(shift_rows)
    ctf_count, half = ctf_table.shape
    img_rows = width // LANES
    slot_rows = img_rows + 16
    rescale = shift_count * poses / images.shape[0]
    rows = shift_count * n
    any_spec = pl.BlockSpec(memory_space=pl.ANY)
    smem = pl.BlockSpec(memory_space=pltpu.SMEM)
    vmem = pl.BlockSpec(memory_space=pltpu.VMEM)
    weights, totals, shifted = pl.pallas_call(
        functools.partial(posterior_kernel, n, (n // 4, 2, 2), rescale),
        out_shape=(
            jax.ShapeDtypeStruct((rows, poses), jnp.bfloat16),
            jax.ShapeDtypeStruct((1, poses), jnp.float32),
            jax.ShapeDtypeStruct((rows, width), jnp.bfloat16),
        ),
        in_specs=[smem, smem, any_spec, any_spec, any_spec, any_spec],
        out_specs=(vmem, vmem, any_spec),
        scratch_shapes=[
            pltpu.VMEM((n, slot_rows, LANES), jnp.bfloat16),
            pltpu.VMEM((n * slot_rows, LANES), jnp.float32),
            pltpu.VMEM((poses, width), jnp.bfloat16),
            pltpu.VMEM((ctf_count, half), jnp.float32),
            pltpu.VMEM((8, half), jnp.float32),
            pltpu.VMEM((rows, width), jnp.bfloat16),
            pltpu.VMEM((n, 2 * n, LANES), jnp.float32),
            pltpu.SemaphoreType.DMA((6,)),
            pltpu.SemaphoreType.DMA,
            pltpu.SemaphoreType.DMA((n,)),
            pltpu.SemaphoreType.DMA((n,)),
            pltpu.SemaphoreType.DMA((n,)),
            pltpu.SemaphoreType.DMA((n,)),
            pltpu.SemaphoreType.DMA,
        ],
        compiler_params=pltpu.CompilerParams(
            collective_id=0, has_side_effects=True, vmem_limit_bytes=40 * 1024 * 1024
        ),
    )(
        ctf_class, tile_mask, images.reshape(img_rows, LANES), projections, ctf_table,
        jnp.asarray(phase_rows(BOX)),
    )
    sums = lax.dot_general(
        weights, shifted, (((0,), (0,)), ((), ())), preferred_element_type=jnp.float32
    )
    return ((rescale * sums).astype(jnp.bfloat16), totals[0])


def fits_fused(n, images, projections, ctf_table, tile_mask):
    poses, width = projections.shape
    return (
        images.shape[0] == 1
        and tile_mask.shape == (1, poses // POSE_TILE)
        and n == IMG_TILE
        and poses <= LANES
        and 3 * ctf_table.shape[0] <= LANES
        and width % (4 * CHUNK) == 0
    )


def per_device(images, ctf_class, projections, ctf_table, tile_mask):
    pose_dev = projections.shape[0]
    img_dev = images.shape[0]
    shift_count = len(shift_rows)
    width_total = projections.shape[1]
    cosine_tab, sine_table = phase_tables(BOX)
    norm_table = norm_terms(projections, ctf_table)
    allowed = jnp.repeat(jnp.repeat(tile_mask, IMG_TILE, axis=0), POSE_TILE, axis=1) > 0

    def shifted_block(pixels, classes, block_index, block_rows):
        pix_block = lax.dynamic_slice_in_dim(pixels, block_index * block_rows, block_rows, 0)
        cls_block = lax.dynamic_slice_in_dim(classes, block_index * block_rows, block_rows, 0)
        stacked = make_shifted(pix_block, cls_block, ctf_table, cosine_tab, sine_table)
        return (stacked.reshape(block_rows * shift_count, width_total), cls_block)

    pieces = (
        lax.all_gather(images, "pose", axis=0, tiled=True),
        lax.all_gather(ctf_class, "pose", axis=0, tiled=True),
    )
    pixels = pieces[0]
    classes = pieces[1]
    row_count = pixels.shape[0]
    block_rows = math.gcd(row_count, 32)

    def score_block(block_index):
        stacked, cls_block = shifted_block(pixels, classes, block_index, block_rows)
        raw_scores = jnp.dot(stacked, projections.T, preferred_element_type=jnp.float32)
        raw_scores = raw_scores.reshape(block_rows, shift_count, pose_dev)
        penalty = jnp.dot(
            class_rows(cls_block, ctf_table.shape[0]), norm_table, precision=lax.Precision.HIGHEST
        )
        return raw_scores - 0.5 * penalty[:, None, :]

    blocks = lax.map(score_block, jnp.arange(row_count // block_rows, dtype=jnp.int32))
    scores = blocks.reshape(row_count, shift_count, pose_dev)
    masked = jnp.where(allowed[:, None, :], scores, floor_score)
    local_peak = jnp.max(masked, axis=(1, 2))
    local_total = jnp.sum(
        jnp.where(allowed[:, None, :], jnp.exp(masked - local_peak[:, None, None]), 0.0),
        axis=(1, 2),
    )
    peak, denominator = joined((local_peak, local_total), "pose", combine_stats)
    exponent = jnp.where(allowed[:, None, :], jnp.exp(masked - peak[:, None, None]), 0.0)
    weights = (exponent / denominator[:, None, None]).astype(jnp.bfloat16)
    empty_sums = jnp.zeros((pose_dev, width_total), jnp.float32)
    pieces = (
        lax.all_gather(images, "pose", axis=0, tiled=True),
        lax.all_gather(ctf_class, "pose", axis=0, tiled=True),
    )
    weighted_pixels = pieces[0]
    weighted_classes = pieces[1]
    row_count = weighted_pixels.shape[0]
    weighted_block_rows = math.gcd(row_count, 32)

    def add_block(block_index, partial_sum):
        stacked, cls_block = shifted_block(
            weighted_pixels, weighted_classes, block_index, weighted_block_rows
        )
        weight_block = lax.dynamic_slice_in_dim(
            weights, block_index * weighted_block_rows, weighted_block_rows, 0
        )
        weight_block = weight_block.reshape(weighted_block_rows * shift_count, pose_dev)
        return partial_sum + lax.dot_general(
            weight_block, stacked, (((0,), (0,)), ((), ())), preferred_element_type=jnp.float32
        )

    accumulated = lax.fori_loop(0, row_count // weighted_block_rows, add_block, empty_sums)
    rescale = shift_count * pose_dev / img_dev
    back_sums = (rescale * accumulated).astype(jnp.bfloat16)
    pose_totals = rescale * jnp.sum(weights.astype(jnp.float32), axis=(0, 1))
    return (back_sums, pose_totals)


def solution(mesh):
    in_specs = (
        P(("groups", "pose"), None),
        P(("groups", "pose")),
        P(("groups", "pose"), None),
        P(),
        P("groups", "pose"),
    )
    out_specs = (P(("groups", "pose"), None), P(("groups", "pose")))
    pose_size = mesh.shape["pose"]

    def body(images, ctf_class, projections, ctf_table, tile_mask):
        if fits_fused(pose_size, images, projections, ctf_table, tile_mask):
            return fused(images, ctf_class, projections, ctf_table, tile_mask, pose_size)
        return per_device(images, ctf_class, projections, ctf_table, tile_mask)

    return jax.shard_map(
        body, mesh=mesh, in_specs=in_specs, out_specs=out_specs, check_vma=False
    )
```

```python
import functools
import math

import jax
import jax.numpy as jnp
import numpy as np
from jax import lax
from jax.experimental import pallas as pl
from jax.experimental.pallas import tpu as pltpu
from jax.sharding import PartitionSpec as P

BOX = 192
IMG_TILE = 16
POSE_TILE = 8


shift_rows = (0.0, 1.0, -1.0, 0.0, 0.0)
shift_cols = (0.0, 0.0, 0.0, 1.0, -1.0)
floor_score = -1e30


def joined(value, axis, join):
    pieces = jax.tree.map(lambda part: lax.all_gather(part, axis), value)
    head = jax.tree.map(lambda part: part[0], pieces)
    tail = jax.tree.map(lambda part: part[1:], pieces)
    running, _ = lax.scan(lambda running, slab: (join(running, slab), None), head, tail)
    return running


def phase_tables(box_size):
    half_box = box_size // 2
    coeff_index = jnp.arange(box_size * half_box, dtype=jnp.int32)
    row_index = coeff_index // half_box
    col_index = coeff_index % half_box
    freq_x = jnp.where(row_index < half_box, row_index, row_index - box_size).astype(jnp.float32)
    freq_y = col_index.astype(jnp.float32)
    step_x = jnp.array(shift_rows, jnp.float32)[:, None]
    step_y = jnp.array(shift_cols, jnp.float32)[:, None]
    phases = 2.0 * math.pi / box_size * (step_x * freq_x[None, :] + step_y * freq_y[None, :])
    return (jnp.cos(phases), jnp.sin(phases))


def class_rows(classes, ctf_count):
    return (classes[:, None] == jnp.arange(ctf_count, dtype=jnp.int32)[None, :]).astype(jnp.float32)


def make_shifted(pixels, classes, ctf_table, cosine_tab, sine_table):
    half_len = pixels.shape[1] // 2
    one_hot = class_rows(classes, ctf_table.shape[0])
    factor = jnp.dot(one_hot, ctf_table, precision=lax.Precision.HIGHEST)[:, None, :]
    real_part = pixels[:, :half_len].astype(jnp.float32)[:, None, :]
    imag_part = pixels[:, half_len:].astype(jnp.float32)[:, None, :]
    shifted_re = (real_part * cosine_tab[None] + imag_part * sine_table[None]) * factor
    shifted_im = (imag_part * cosine_tab[None] - real_part * sine_table[None]) * factor
    return jnp.concatenate([shifted_re, shifted_im], axis=2).astype(jnp.bfloat16)


def norm_terms(projections, ctf_table):
    squared = ctf_table * ctf_table
    squared = jnp.concatenate([squared, squared], axis=1)
    proj_f = projections.astype(jnp.float32)
    return jnp.dot(squared, (proj_f * proj_f).T, precision=lax.Precision.HIGHEST)


def combine_stats(earlier, latter):
    highest = jnp.maximum(earlier[0], latter[0])
    return (
        highest,
        earlier[1] * jnp.exp(earlier[0] - highest) + latter[1] * jnp.exp(latter[0] - highest),
    )


LANES = 128
CHUNK = 1024
NT = (((1,), (1,)), ((), ()))


def phase_rows(box_size):
    half_box = box_size // 2
    coeff_index = np.arange(box_size * half_box)
    row_index = coeff_index // half_box
    freq_x = np.where(row_index < half_box, row_index, row_index - box_size)
    freq_y = coeff_index % half_box
    turn = 2.0 * math.pi / box_size
    rows = [np.cos(turn * freq_x), np.sin(turn * freq_x), np.cos(turn * freq_y), np.sin(turn * freq_y)]
    return np.stack(rows + rows).astype(np.float32)


def split_bf16(value, pieces):
    parts = []
    for _ in range(pieces):
        part = value.astype(jnp.bfloat16)
        parts.append(part)
        value = value - part.astype(jnp.float32)
    return jnp.concatenate(parts, axis=0)


def posterior_kernel(
    n, factors, rescale, cls_ref, mask_ref, img_hbm, proj_hbm, ctf_hbm, tab_hbm,
    weights_ref, totals_ref, shifted_hbm,
    slots, imgf, proj, ctf, tab, shifted, stats,
    load_sem, img_sem, send_sem, recv_sem, stat_send, stat_recv, out_sem,
):
    nz, ny, nc = factors
    me = lax.axis_index("pose")
    core = lax.rem(me, nc)
    row = lax.rem(lax.div(me, nc), ny)
    deep = lax.div(me, nc * ny)

    def device(z, y, c):
        return (z * ny + y) * nc + c

    poses, width = proj.shape
    half = width // 2
    quarter = half // 2
    img_rows = width // LANES
    slot_rows = slots.shape[1]
    ctf_count = ctf.shape[0]

    loads = [
        pltpu.make_async_copy(ctf_hbm, ctf, load_sem.at[0]),
        pltpu.make_async_copy(tab_hbm, tab, load_sem.at[1]),
    ]
    for j in range(4):
        cols = pl.ds(((j % 2) * 2 + j // 2) * quarter, quarter)
        loads.append(
            pltpu.make_async_copy(proj_hbm.at[:, cols], proj.at[:, cols], load_sem.at[2 + j])
        )
    own = pltpu.make_async_copy(img_hbm, slots.at[me, pl.ds(0, img_rows)], img_sem)
    own.start()
    for copy in (loads[0], loads[2], loads[3], loads[4], loads[5], loads[1]):
        copy.start()
    barrier = pltpu.get_barrier_semaphore()
    for d in range(1, n):
        pl.semaphore_signal(
            barrier, inc=1, device_id={"pose": lax.rem(me + d, n)},
            device_id_type=pl.DeviceIdType.MESH,
        )
    label = cls_ref[0].astype(jnp.float32)
    slots[me, pl.ds(img_rows, slot_rows - img_rows), :] = jnp.full(
        (slot_rows - img_rows, LANES), label, jnp.float32
    ).astype(jnp.bfloat16)
    own.wait()
    pl.semaphore_wait(barrier, n - 1)

    started = []
    cut = slot_rows // 32 * 16
    pieces = ((0, cut), (cut, slot_rows - cut))

    def image_copy(owner, piece, target, slot):
        part = slots.at[owner, pl.ds(*pieces[piece])]
        return pltpu.make_async_remote_copy(
            src_ref=part, dst_ref=part,
            send_sem=send_sem.at[slot], recv_sem=recv_sem.at[owner, piece],
            device_id={"pose": target}, device_id_type=pl.DeviceIdType.MESH,
        )

    def send(owner, piece, target, *needs):
        copy = image_copy(owner, piece, target, len(started))
        started.append((copy, needs))
        run_if(needs, copy.start)

    def run_if(needs, action):
        if needs:
            pl.when(functools.reduce(jnp.logical_and, needs))(action)
        else:
            action()

    def arrive(owner, piece, *needs):
        run_if(needs, image_copy(owner, piece, me, 0).wait_recv)

    across = device(deep, lax.rem(row + 1, ny), core)
    beside = device(deep, row, lax.rem(core + 1, nc))
    up_ok, down_ok = deep + 1 < nz, deep >= 1
    up = device(jnp.minimum(deep + 1, nz - 1), row, core)
    down = device(jnp.maximum(deep - 1, 0), row, core)
    for piece in range(2):
        send(me, piece, up, up_ok)
        send(me, piece, down, down_ok)
        send(me, piece, across)
    for piece in range(2):
        send(me, piece, beside)

    def line_event(d):
        below, above = deep - d >= 0, deep + d < nz
        low = device(jnp.maximum(deep - d, 0), row, core)
        high = device(jnp.minimum(deep + d, nz - 1), row, core)
        for piece in range(2):
            arrive(low, piece, below)
            if d < nz - 1:
                send(low, piece, up, below, up_ok)
            send(low, piece, across, below)
            arrive(high, piece, above)
            if d < nz - 1:
                send(high, piece, down, above, down_ok)
            send(high, piece, across, above)
        for piece in range(2):
            send(low, piece, beside, below)
            send(high, piece, beside, above)

    def across_event(d):
        other = lax.rem(row + 1, ny)
        if d == 0:
            for piece in range(2):
                arrive(across, piece)
                send(across, piece, beside)
            return
        below, above = deep - d >= 0, deep + d < nz
        low = device(jnp.maximum(deep - d, 0), other, core)
        high = device(jnp.minimum(deep + d, nz - 1), other, core)
        for piece in range(2):
            arrive(low, piece, below)
            send(low, piece, beside, below)
            arrive(high, piece, above)
            send(high, piece, beside, above)

    def norm_step(j, total):
        start = pl.multiple_of(j * CHUNK, CHUNK)
        real = proj[:, pl.ds(start, CHUNK)].astype(jnp.float32)
        imag = proj[:, pl.ds(pl.multiple_of(start + half, CHUNK), CHUNK)].astype(jnp.float32)
        gain = ctf[:, pl.ds(start, CHUNK)]
        power = split_bf16(real * real + imag * imag, 2)
        return total + lax.dot_general(
            split_bf16(gain * gain, 2), power, NT, preferred_element_type=jnp.float32
        )

    steps = half // CHUNK
    events = []
    for d in range(1, nz):
        events += [functools.partial(line_event, d), functools.partial(across_event, d - 1)]
    events.append(functools.partial(across_event, nz - 1))
    for copy in loads[:1] + loads[2:]:
        copy.wait()
    norm = jnp.zeros((2 * ctf_count, 2 * poses), jnp.float32)
    for e in range(len(events) + 1):
        bounds = [steps * k // (len(events) + 1) for k in (e, e + 1)]
        norm = lax.fori_loop(*bounds, norm_step, norm)
        if e < len(events):
            events[e]()
    norm = norm[:ctf_count] + norm[ctf_count:]
    norm = norm[:, :poses] + norm[:, poses:]
    loads[1].wait()
    for y in range(ny):
        for z in range(nz):
            for piece in range(2):
                arrive(device(z, y, lax.rem(core + 1, nc)), piece)

    def widen(i, carry):
        imgf[pl.ds(pl.multiple_of(i * slot_rows, 16), slot_rows), :] = slots[i].astype(jnp.float32)
        return carry

    lax.fori_loop(0, n, widen, 0)
    labels = imgf[pl.ds(img_rows, n, stride=slot_rows), :]
    lanes = lax.broadcasted_iota(jnp.int32, (n, LANES), 1)
    one_hot = (labels == lax.rem(lanes, ctf_count).astype(jnp.float32)).astype(jnp.float32)
    picker = one_hot[:, : 3 * ctf_count].astype(jnp.bfloat16)
    half_rows = half // LANES

    def shift_step(j, total):
        start = pl.multiple_of(j * CHUNK, CHUNK)
        later = pl.multiple_of(start + half, CHUNK)
        gain = jnp.dot(
            picker, split_bf16(ctf[:, pl.ds(start, CHUNK)], 3), preferred_element_type=jnp.float32
        )
        for k in range(CHUNK // LANES):
            at = j * (CHUNK // LANES) + k
            cols = slice(k * LANES, (k + 1) * LANES)
            place = pl.ds(pl.multiple_of(start + k * LANES, LANES), LANES)
            place_im = pl.ds(pl.multiple_of(later + k * LANES, LANES), LANES)
            factor = gain[:, cols]
            real = imgf[pl.ds(at, n, stride=slot_rows), :] * factor
            imag = imgf[pl.ds(at + half_rows, n, stride=slot_rows), :] * factor
            shifted[0:n, place] = real.astype(jnp.bfloat16)
            shifted[0:n, place_im] = imag.astype(jnp.bfloat16)
            for axis in range(2):
                cosine = tab[2 * axis : 2 * axis + 1, place]
                sine = tab[2 * axis + 1 : 2 * axis + 2, place]
                first, second = real * cosine, imag * sine
                third, fourth = imag * cosine, real * sine
                low = (2 * axis + 1) * n
                shifted[low : low + n, place] = (first + second).astype(jnp.bfloat16)
                shifted[low : low + n, place_im] = (third - fourth).astype(jnp.bfloat16)
                shifted[low + n : low + 2 * n, place] = (first - second).astype(jnp.bfloat16)
                shifted[low + n : low + 2 * n, place_im] = (third + fourth).astype(jnp.bfloat16)
        for begin in (start, later):
            total = total + lax.dot_general(
                shifted[:, pl.ds(begin, CHUNK)], proj[:, pl.ds(begin, CHUNK)], NT,
                preferred_element_type=jnp.float32,
            )
        return total

    shift_count = shifted.shape[0] // n
    raw = jnp.zeros((shift_count * n, poses), jnp.float32)
    written = []
    for part in range(3):
        bounds = [steps * k // 3 for k in (part, part + 1)]
        raw = lax.fori_loop(*bounds, shift_step, raw)
        for base in (0, half):
            cols = pl.ds(base + bounds[0] * CHUNK, (bounds[1] - bounds[0]) * CHUNK)
            copy = pltpu.make_async_copy(
                shifted.at[:, cols], shifted_hbm.at[:, cols], out_sem.at[len(written)]
            )
            copy.start()
            written.append(copy)

    penalty = 0.5 * jnp.dot(
        one_hot[:, :ctf_count], norm,
        precision=lax.Precision.HIGHEST, preferred_element_type=jnp.float32,
    )
    tile = lax.div(lax.broadcasted_iota(jnp.int32, (n, poses), 1), POSE_TILE)
    allowed = jnp.zeros((n, poses), jnp.int32)
    for j in range(poses // POSE_TILE):
        allowed = jnp.where(tile == j, mask_ref[0, j], allowed)
    allowed = allowed > 0
    masked = [
        jnp.where(allowed, raw[t * n : (t + 1) * n] - penalty, floor_score)
        for t in range(shift_count)
    ]
    highest = functools.reduce(jnp.maximum, masked)
    peak = jnp.max(highest, axis=1, keepdims=True)
    mass = sum(jnp.where(allowed, jnp.exp(part - peak), 0.0) for part in masked)
    mass = jnp.sum(mass, axis=1, keepdims=True)
    stats[me, 0:n, :] = jnp.broadcast_to(peak, (n, LANES))
    stats[me, n : 2 * n, :] = jnp.broadcast_to(mass, (n, LANES))

    def stat_copy(owner, target, slot):
        return pltpu.make_async_remote_copy(
            src_ref=stats.at[owner], dst_ref=stats.at[owner],
            send_sem=stat_send.at[slot], recv_sem=stat_recv.at[owner],
            device_id={"pose": target}, device_id_type=pl.DeviceIdType.MESH,
        )

    sent = [stat_copy(me, lax.rem(me + d, n), d - 1) for d in range(1, n)]
    for copy in sent:
        copy.start()
    for d in range(1, n):
        stat_copy(lax.rem(me + d, n), me, d - 1).wait_recv()
    top = functools.reduce(jnp.maximum, [stats[j, 0:n, :] for j in range(n)])
    total = sum(stats[j, n : 2 * n, :] * jnp.exp(stats[j, 0:n, :] - top) for j in range(n))
    top = top[:, :poses]
    total = total[:, :poses]
    column = jnp.zeros((n, poses), jnp.float32)
    for t in range(shift_count):
        weight = jnp.where(allowed, jnp.exp(masked[t] - top), 0.0) / total
        weight = weight.astype(jnp.bfloat16)
        weights_ref[t * n : (t + 1) * n, :] = weight
        column = column + weight.astype(jnp.float32)
    totals_ref[...] = rescale * jnp.sum(column, axis=0, keepdims=True)
    for copy, needs in started:
        run_if(needs, copy.wait_send)
    for copy in sent:
        copy.wait_send()
    for copy in written:
        copy.wait()


def fused(images, ctf_class, projections, ctf_table, tile_mask, n):
    poses, width = projections.shape
    shift_count = len(shift_rows)
    ctf_count, half = ctf_table.shape
    img_rows = width // LANES
    slot_rows = img_rows + 16
    rescale = shift_count * poses / images.shape[0]
    rows = shift_count * n
    any_spec = pl.BlockSpec(memory_space=pl.ANY)
    smem = pl.BlockSpec(memory_space=pltpu.SMEM)
    vmem = pl.BlockSpec(memory_space=pltpu.VMEM)
    weights, totals, shifted = pl.pallas_call(
        functools.partial(posterior_kernel, n, (n // 4, 2, 2), rescale),
        out_shape=(
            jax.ShapeDtypeStruct((rows, poses), jnp.bfloat16),
            jax.ShapeDtypeStruct((1, poses), jnp.float32),
            jax.ShapeDtypeStruct((rows, width), jnp.bfloat16),
        ),
        in_specs=[smem, smem, any_spec, any_spec, any_spec, any_spec],
        out_specs=(vmem, vmem, any_spec),
        scratch_shapes=[
            pltpu.VMEM((n, slot_rows, LANES), jnp.bfloat16),
            pltpu.VMEM((n * slot_rows, LANES), jnp.float32),
            pltpu.VMEM((poses, width), jnp.bfloat16),
            pltpu.VMEM((ctf_count, half), jnp.float32),
            pltpu.VMEM((8, half), jnp.float32),
            pltpu.VMEM((rows, width), jnp.bfloat16),
            pltpu.VMEM((n, 2 * n, LANES), jnp.float32),
            pltpu.SemaphoreType.DMA((6,)),
            pltpu.SemaphoreType.DMA,
            pltpu.SemaphoreType.DMA((8 * n,)),
            pltpu.SemaphoreType.DMA((n, 2)),
            pltpu.SemaphoreType.DMA((n,)),
            pltpu.SemaphoreType.DMA((n,)),
            pltpu.SemaphoreType.DMA((6,)),
        ],
        compiler_params=pltpu.CompilerParams(
            collective_id=0, has_side_effects=True, vmem_limit_bytes=60 * 1024 * 1024
        ),
    )(
        ctf_class, tile_mask, images.reshape(img_rows, LANES), projections, ctf_table,
        jnp.asarray(phase_rows(BOX)),
    )
    sums = lax.dot_general(
        weights, shifted, (((0,), (0,)), ((), ())), preferred_element_type=jnp.float32
    )
    return ((rescale * sums).astype(jnp.bfloat16), totals[0])


def fits_fused(n, images, projections, ctf_table, tile_mask):
    poses, width = projections.shape
    return (
        images.shape[0] == 1
        and tile_mask.shape == (1, poses // POSE_TILE)
        and n == IMG_TILE
        and poses <= LANES
        and 3 * ctf_table.shape[0] <= LANES
        and width % (4 * CHUNK) == 0
    )


def per_device(images, ctf_class, projections, ctf_table, tile_mask):
    pose_dev = projections.shape[0]
    img_dev = images.shape[0]
    shift_count = len(shift_rows)
    width_total = projections.shape[1]
    cosine_tab, sine_table = phase_tables(BOX)
    norm_table = norm_terms(projections, ctf_table)
    allowed = jnp.repeat(jnp.repeat(tile_mask, IMG_TILE, axis=0), POSE_TILE, axis=1) > 0

    def shifted_block(pixels, classes, block_index, block_rows):
        pix_block = lax.dynamic_slice_in_dim(pixels, block_index * block_rows, block_rows, 0)
        cls_block = lax.dynamic_slice_in_dim(classes, block_index * block_rows, block_rows, 0)
        stacked = make_shifted(pix_block, cls_block, ctf_table, cosine_tab, sine_table)
        return (stacked.reshape(block_rows * shift_count, width_total), cls_block)

    pieces = (
        lax.all_gather(images, "pose", axis=0, tiled=True),
        lax.all_gather(ctf_class, "pose", axis=0, tiled=True),
    )
    pixels = pieces[0]
    classes = pieces[1]
    row_count = pixels.shape[0]
    block_rows = math.gcd(row_count, 32)

    def score_block(block_index):
        stacked, cls_block = shifted_block(pixels, classes, block_index, block_rows)
        raw_scores = jnp.dot(stacked, projections.T, preferred_element_type=jnp.float32)
        raw_scores = raw_scores.reshape(block_rows, shift_count, pose_dev)
        penalty = jnp.dot(
            class_rows(cls_block, ctf_table.shape[0]), norm_table, precision=lax.Precision.HIGHEST
        )
        return raw_scores - 0.5 * penalty[:, None, :]

    blocks = lax.map(score_block, jnp.arange(row_count // block_rows, dtype=jnp.int32))
    scores = blocks.reshape(row_count, shift_count, pose_dev)
    masked = jnp.where(allowed[:, None, :], scores, floor_score)
    local_peak = jnp.max(masked, axis=(1, 2))
    local_total = jnp.sum(
        jnp.where(allowed[:, None, :], jnp.exp(masked - local_peak[:, None, None]), 0.0),
        axis=(1, 2),
    )
    peak, denominator = joined((local_peak, local_total), "pose", combine_stats)
    exponent = jnp.where(allowed[:, None, :], jnp.exp(masked - peak[:, None, None]), 0.0)
    weights = (exponent / denominator[:, None, None]).astype(jnp.bfloat16)
    empty_sums = jnp.zeros((pose_dev, width_total), jnp.float32)
    pieces = (
        lax.all_gather(images, "pose", axis=0, tiled=True),
        lax.all_gather(ctf_class, "pose", axis=0, tiled=True),
    )
    weighted_pixels = pieces[0]
    weighted_classes = pieces[1]
    row_count = weighted_pixels.shape[0]
    weighted_block_rows = math.gcd(row_count, 32)

    def add_block(block_index, partial_sum):
        stacked, cls_block = shifted_block(
            weighted_pixels, weighted_classes, block_index, weighted_block_rows
        )
        weight_block = lax.dynamic_slice_in_dim(
            weights, block_index * weighted_block_rows, weighted_block_rows, 0
        )
        weight_block = weight_block.reshape(weighted_block_rows * shift_count, pose_dev)
        return partial_sum + lax.dot_general(
            weight_block, stacked, (((0,), (0,)), ((), ())), preferred_element_type=jnp.float32
        )

    accumulated = lax.fori_loop(0, row_count // weighted_block_rows, add_block, empty_sums)
    rescale = shift_count * pose_dev / img_dev
    back_sums = (rescale * accumulated).astype(jnp.bfloat16)
    pose_totals = rescale * jnp.sum(weights.astype(jnp.float32), axis=(0, 1))
    return (back_sums, pose_totals)


def solution(mesh):
    in_specs = (
        P(("groups", "pose"), None),
        P(("groups", "pose")),
        P(("groups", "pose"), None),
        P(),
        P("groups", "pose"),
    )
    out_specs = (P(("groups", "pose"), None), P(("groups", "pose")))
    pose_size = mesh.shape["pose"]

    def body(images, ctf_class, projections, ctf_table, tile_mask):
        if fits_fused(pose_size, images, projections, ctf_table, tile_mask):
            return fused(images, ctf_class, projections, ctf_table, tile_mask, pose_size)
        return per_device(images, ctf_class, projections, ctf_table, tile_mask)

    return jax.shard_map(
        body, mesh=mesh, in_specs=in_specs, out_specs=out_specs, check_vma=False
    )
```

```python
import functools
import math

import jax
import jax.numpy as jnp
import numpy as np
from jax import lax
from jax.experimental import pallas as pl
from jax.experimental.pallas import tpu as pltpu
from jax.sharding import PartitionSpec as P

BOX = 192
IMG_TILE = 16
POSE_TILE = 8


shift_rows = (0.0, 1.0, -1.0, 0.0, 0.0)
shift_cols = (0.0, 0.0, 0.0, 1.0, -1.0)
floor_score = -1e30


def joined(value, axis, join):
    pieces = jax.tree.map(lambda part: lax.all_gather(part, axis), value)
    head = jax.tree.map(lambda part: part[0], pieces)
    tail = jax.tree.map(lambda part: part[1:], pieces)
    running, _ = lax.scan(lambda running, slab: (join(running, slab), None), head, tail)
    return running


def phase_tables(box_size):
    half_box = box_size // 2
    coeff_index = jnp.arange(box_size * half_box, dtype=jnp.int32)
    row_index = coeff_index // half_box
    col_index = coeff_index % half_box
    freq_x = jnp.where(row_index < half_box, row_index, row_index - box_size).astype(jnp.float32)
    freq_y = col_index.astype(jnp.float32)
    step_x = jnp.array(shift_rows, jnp.float32)[:, None]
    step_y = jnp.array(shift_cols, jnp.float32)[:, None]
    phases = 2.0 * math.pi / box_size * (step_x * freq_x[None, :] + step_y * freq_y[None, :])
    return (jnp.cos(phases), jnp.sin(phases))


def class_rows(classes, ctf_count):
    return (classes[:, None] == jnp.arange(ctf_count, dtype=jnp.int32)[None, :]).astype(jnp.float32)


def make_shifted(pixels, classes, ctf_table, cosine_tab, sine_table):
    half_len = pixels.shape[1] // 2
    one_hot = class_rows(classes, ctf_table.shape[0])
    factor = jnp.dot(one_hot, ctf_table, precision=lax.Precision.HIGHEST)[:, None, :]
    real_part = pixels[:, :half_len].astype(jnp.float32)[:, None, :]
    imag_part = pixels[:, half_len:].astype(jnp.float32)[:, None, :]
    shifted_re = (real_part * cosine_tab[None] + imag_part * sine_table[None]) * factor
    shifted_im = (imag_part * cosine_tab[None] - real_part * sine_table[None]) * factor
    return jnp.concatenate([shifted_re, shifted_im], axis=2).astype(jnp.bfloat16)


def norm_terms(projections, ctf_table):
    squared = ctf_table * ctf_table
    squared = jnp.concatenate([squared, squared], axis=1)
    proj_f = projections.astype(jnp.float32)
    return jnp.dot(squared, (proj_f * proj_f).T, precision=lax.Precision.HIGHEST)


def combine_stats(earlier, latter):
    highest = jnp.maximum(earlier[0], latter[0])
    return (
        highest,
        earlier[1] * jnp.exp(earlier[0] - highest) + latter[1] * jnp.exp(latter[0] - highest),
    )


LANES = 128
CHUNK = 1024
NT = (((1,), (1,)), ((), ()))


def phase_rows(box_size):
    half_box = box_size // 2
    coeff_index = np.arange(box_size * half_box)
    row_index = coeff_index // half_box
    freq_x = np.where(row_index < half_box, row_index, row_index - box_size)
    freq_y = coeff_index % half_box
    turn = 2.0 * math.pi / box_size
    rows = [np.cos(turn * freq_x), np.sin(turn * freq_x), np.cos(turn * freq_y), np.sin(turn * freq_y)]
    return np.stack(rows + rows).astype(np.float32)


def split_bf16(value, pieces):
    parts = []
    for _ in range(pieces):
        part = value.astype(jnp.bfloat16)
        parts.append(part)
        value = value - part.astype(jnp.float32)
    return jnp.concatenate(parts, axis=0)


def posterior_kernel(
    n, factors, rescale, cls_ref, mask_ref, img_hbm, proj_hbm, ctf_hbm, tab_hbm,
    weights_ref, totals_ref, shifted_hbm,
    slots, imgf, proj, ctf, tab, shifted, stats,
    load_sem, img_sem, send_sem, recv_sem, stat_send, stat_recv, out_sem,
):
    nz, ny, nc = factors
    me = lax.axis_index("pose")
    core = lax.rem(me, nc)
    row = lax.rem(lax.div(me, nc), ny)
    deep = lax.div(me, nc * ny)

    def device(z, y, c):
        return (z * ny + y) * nc + c

    poses, width = proj.shape
    half = width // 2
    quarter = half // 2
    img_rows = width // LANES
    slot_rows = slots.shape[1]
    ctf_count = ctf.shape[0]

    loads = [
        pltpu.make_async_copy(ctf_hbm, ctf, load_sem.at[0]),
        pltpu.make_async_copy(tab_hbm, tab, load_sem.at[1]),
    ]
    for j in range(4):
        cols = pl.ds(((j % 2) * 2 + j // 2) * quarter, quarter)
        loads.append(
            pltpu.make_async_copy(proj_hbm.at[:, cols], proj.at[:, cols], load_sem.at[2 + j])
        )
    own = pltpu.make_async_copy(img_hbm, slots.at[me, pl.ds(0, img_rows)], img_sem)
    own.start()
    for copy in (loads[0], loads[2], loads[3], loads[4], loads[5], loads[1]):
        copy.start()
    barrier = pltpu.get_barrier_semaphore()
    for d in range(1, n):
        pl.semaphore_signal(
            barrier, inc=1, device_id={"pose": lax.rem(me + d, n)},
            device_id_type=pl.DeviceIdType.MESH,
        )
    label = cls_ref[0].astype(jnp.float32)
    slots[me, pl.ds(img_rows, slot_rows - img_rows), :] = jnp.full(
        (slot_rows - img_rows, LANES), label, jnp.float32
    ).astype(jnp.bfloat16)
    own.wait()
    pl.semaphore_wait(barrier, n - 1)

    started = []
    cut = slot_rows // 32 * 16
    pieces = ((0, cut), (cut, slot_rows - cut))

    def image_copy(owner, piece, target, slot):
        part = slots.at[owner, pl.ds(*pieces[piece])]
        return pltpu.make_async_remote_copy(
            src_ref=part, dst_ref=part,
            send_sem=send_sem.at[slot], recv_sem=recv_sem.at[owner, piece],
            device_id={"pose": target}, device_id_type=pl.DeviceIdType.MESH,
        )

    def send(owner, piece, target, *needs):
        copy = image_copy(owner, piece, target, len(started))
        started.append((copy, needs))
        run_if(needs, copy.start)

    def run_if(needs, action):
        if needs:
            pl.when(functools.reduce(jnp.logical_and, needs))(action)
        else:
            action()

    def arrive(owner, piece, *needs):
        run_if(needs, image_copy(owner, piece, me, 0).wait_recv)

    across = device(deep, lax.rem(row + 1, ny), core)
    beside = device(deep, row, lax.rem(core + 1, nc))
    up_ok, down_ok = deep + 1 < nz, deep >= 1
    up = device(jnp.minimum(deep + 1, nz - 1), row, core)
    down = device(jnp.maximum(deep - 1, 0), row, core)
    for piece in range(2):
        send(me, piece, up, up_ok)
        send(me, piece, down, down_ok)
        send(me, piece, across)
    for piece in range(2):
        send(me, piece, beside)

    def line_event(d):
        below, above = deep - d >= 0, deep + d < nz
        low = device(jnp.maximum(deep - d, 0), row, core)
        high = device(jnp.minimum(deep + d, nz - 1), row, core)
        for piece in range(2):
            arrive(low, piece, below)
            if d < nz - 1:
                send(low, piece, up, below, up_ok)
            send(low, piece, across, below)
            arrive(high, piece, above)
            if d < nz - 1:
                send(high, piece, down, above, down_ok)
            send(high, piece, across, above)
        for piece in range(2):
            send(low, piece, beside, below)
            send(high, piece, beside, above)

    def across_event(d):
        other = lax.rem(row + 1, ny)
        if d == 0:
            for piece in range(2):
                arrive(across, piece)
                send(across, piece, beside)
            return
        below, above = deep - d >= 0, deep + d < nz
        low = device(jnp.maximum(deep - d, 0), other, core)
        high = device(jnp.minimum(deep + d, nz - 1), other, core)
        for piece in range(2):
            arrive(low, piece, below)
            send(low, piece, beside, below)
            arrive(high, piece, above)
            send(high, piece, beside, above)

    def norm_step(j, total):
        start = pl.multiple_of(j * CHUNK, CHUNK)
        real = proj[:, pl.ds(start, CHUNK)].astype(jnp.float32)
        imag = proj[:, pl.ds(pl.multiple_of(start + half, CHUNK), CHUNK)].astype(jnp.float32)
        gain = ctf[:, pl.ds(start, CHUNK)]
        power = split_bf16(real * real + imag * imag, 2)
        return total + lax.dot_general(
            split_bf16(gain * gain, 2), power, NT, preferred_element_type=jnp.float32
        )

    steps = half // CHUNK
    events = []
    for d in range(1, nz):
        events += [functools.partial(line_event, d), functools.partial(across_event, d - 1)]
    events.append(functools.partial(across_event, nz - 1))
    for copy in loads[:1] + loads[2:]:
        copy.wait()
    norm = jnp.zeros((2 * ctf_count, 2 * poses), jnp.float32)
    for e in range(len(events) + 1):
        bounds = [steps * k // (len(events) + 1) for k in (e, e + 1)]
        norm = lax.fori_loop(*bounds, norm_step, norm)
        if e < len(events):
            events[e]()
    norm = norm[:ctf_count] + norm[ctf_count:]
    norm = norm[:, :poses] + norm[:, poses:]
    loads[1].wait()
    for y in range(ny):
        for z in range(nz):
            for piece in range(2):
                arrive(device(z, y, lax.rem(core + 1, nc)), piece)

    def widen(i, carry):
        imgf[pl.ds(pl.multiple_of(i * slot_rows, 16), slot_rows), :] = slots[i].astype(jnp.float32)
        return carry

    lax.fori_loop(0, n, widen, 0)
    labels = imgf[pl.ds(img_rows, n, stride=slot_rows), :]
    lanes = lax.broadcasted_iota(jnp.int32, (n, LANES), 1)
    one_hot = (labels == lax.rem(lanes, ctf_count).astype(jnp.float32)).astype(jnp.float32)
    picker = one_hot[:, : 3 * ctf_count].astype(jnp.bfloat16)
    half_rows = half // LANES

    def score_step(j, total):
        start = pl.multiple_of(j * CHUNK, CHUNK)
        for begin in (start, pl.multiple_of(start + half, CHUNK)):
            total = total + lax.dot_general(
                shifted[:, pl.ds(begin, CHUNK)], proj[:, pl.ds(begin, CHUNK)], NT,
                preferred_element_type=jnp.float32,
            )
        return total

    def shift_step(j, total):
        total = score_step(j - 1, total)
        fill_step(j)
        return total

    def fill_step(j):
        start = pl.multiple_of(j * CHUNK, CHUNK)
        later = pl.multiple_of(start + half, CHUNK)
        gain = jnp.dot(
            picker, split_bf16(ctf[:, pl.ds(start, CHUNK)], 3), preferred_element_type=jnp.float32
        )
        for k in range(CHUNK // LANES):
            at = j * (CHUNK // LANES) + k
            cols = slice(k * LANES, (k + 1) * LANES)
            place = pl.ds(pl.multiple_of(start + k * LANES, LANES), LANES)
            place_im = pl.ds(pl.multiple_of(later + k * LANES, LANES), LANES)
            factor = gain[:, cols]
            real = imgf[pl.ds(at, n, stride=slot_rows), :] * factor
            imag = imgf[pl.ds(at + half_rows, n, stride=slot_rows), :] * factor
            shifted[0:n, place] = real.astype(jnp.bfloat16)
            shifted[0:n, place_im] = imag.astype(jnp.bfloat16)
            for axis in range(2):
                cosine = tab[2 * axis : 2 * axis + 1, place]
                sine = tab[2 * axis + 1 : 2 * axis + 2, place]
                first, second = real * cosine, imag * sine
                third, fourth = imag * cosine, real * sine
                low = (2 * axis + 1) * n
                shifted[low : low + n, place] = (first + second).astype(jnp.bfloat16)
                shifted[low : low + n, place_im] = (third - fourth).astype(jnp.bfloat16)
                shifted[low + n : low + 2 * n, place] = (first - second).astype(jnp.bfloat16)
                shifted[low + n : low + 2 * n, place_im] = (third + fourth).astype(jnp.bfloat16)

    shift_count = shifted.shape[0] // n
    raw = jnp.zeros((shift_count * n, poses), jnp.float32)
    written = []
    fill_step(0)
    for part in range(3):
        bounds = [steps * k // 3 for k in (part, part + 1)]
        raw = lax.fori_loop(max(bounds[0], 1), bounds[1], shift_step, raw)
        for base in (0, half):
            cols = pl.ds(base + bounds[0] * CHUNK, (bounds[1] - bounds[0]) * CHUNK)
            copy = pltpu.make_async_copy(
                shifted.at[:, cols], shifted_hbm.at[:, cols], out_sem.at[len(written)]
            )
            copy.start()
            written.append(copy)
    raw = score_step(steps - 1, raw)

    penalty = 0.5 * jnp.dot(
        one_hot[:, :ctf_count], norm,
        precision=lax.Precision.HIGHEST, preferred_element_type=jnp.float32,
    )
    tile = lax.div(lax.broadcasted_iota(jnp.int32, (n, poses), 1), POSE_TILE)
    allowed = jnp.zeros((n, poses), jnp.int32)
    for j in range(poses // POSE_TILE):
        allowed = jnp.where(tile == j, mask_ref[0, j], allowed)
    allowed = allowed > 0
    masked = [
        jnp.where(allowed, raw[t * n : (t + 1) * n] - penalty, floor_score)
        for t in range(shift_count)
    ]
    highest = functools.reduce(jnp.maximum, masked)
    peak = jnp.max(highest, axis=1, keepdims=True)
    mass = sum(jnp.where(allowed, jnp.exp(part - peak), 0.0) for part in masked)
    mass = jnp.sum(mass, axis=1, keepdims=True)
    stats[me, 0:n, :] = jnp.broadcast_to(peak, (n, LANES))
    stats[me, n : 2 * n, :] = jnp.broadcast_to(mass, (n, LANES))

    def stat_copy(owner, target, slot):
        return pltpu.make_async_remote_copy(
            src_ref=stats.at[owner], dst_ref=stats.at[owner],
            send_sem=stat_send.at[slot], recv_sem=stat_recv.at[owner],
            device_id={"pose": target}, device_id_type=pl.DeviceIdType.MESH,
        )

    sent = [stat_copy(me, lax.rem(me + d, n), d - 1) for d in range(1, n)]
    for copy in sent:
        copy.start()
    for d in range(1, n):
        stat_copy(lax.rem(me + d, n), me, d - 1).wait_recv()
    top = functools.reduce(jnp.maximum, [stats[j, 0:n, :] for j in range(n)])
    total = sum(stats[j, n : 2 * n, :] * jnp.exp(stats[j, 0:n, :] - top) for j in range(n))
    top = top[:, :poses]
    total = total[:, :poses]
    column = jnp.zeros((n, poses), jnp.float32)
    for t in range(shift_count):
        weight = jnp.where(allowed, jnp.exp(masked[t] - top), 0.0) / total
        weight = weight.astype(jnp.bfloat16)
        weights_ref[t * n : (t + 1) * n, :] = weight
        column = column + weight.astype(jnp.float32)
    totals_ref[...] = rescale * jnp.sum(column, axis=0, keepdims=True)
    for copy, needs in started:
        run_if(needs, copy.wait_send)
    for copy in sent:
        copy.wait_send()
    for copy in written:
        copy.wait()


def fused(images, ctf_class, projections, ctf_table, tile_mask, n):
    poses, width = projections.shape
    shift_count = len(shift_rows)
    ctf_count, half = ctf_table.shape
    img_rows = width // LANES
    slot_rows = img_rows + 16
    rescale = shift_count * poses / images.shape[0]
    rows = shift_count * n
    any_spec = pl.BlockSpec(memory_space=pl.ANY)
    smem = pl.BlockSpec(memory_space=pltpu.SMEM)
    vmem = pl.BlockSpec(memory_space=pltpu.VMEM)
    weights, totals, shifted = pl.pallas_call(
        functools.partial(posterior_kernel, n, (n // 4, 2, 2), rescale),
        out_shape=(
            jax.ShapeDtypeStruct((rows, poses), jnp.bfloat16),
            jax.ShapeDtypeStruct((1, poses), jnp.float32),
            jax.ShapeDtypeStruct((rows, width), jnp.bfloat16),
        ),
        in_specs=[smem, smem, any_spec, any_spec, any_spec, any_spec],
        out_specs=(vmem, vmem, any_spec),
        scratch_shapes=[
            pltpu.VMEM((n, slot_rows, LANES), jnp.bfloat16),
            pltpu.VMEM((n * slot_rows, LANES), jnp.float32),
            pltpu.VMEM((poses, width), jnp.bfloat16),
            pltpu.VMEM((ctf_count, half), jnp.float32),
            pltpu.VMEM((8, half), jnp.float32),
            pltpu.VMEM((rows, width), jnp.bfloat16),
            pltpu.VMEM((n, 2 * n, LANES), jnp.float32),
            pltpu.SemaphoreType.DMA((6,)),
            pltpu.SemaphoreType.DMA,
            pltpu.SemaphoreType.DMA((8 * n,)),
            pltpu.SemaphoreType.DMA((n, 2)),
            pltpu.SemaphoreType.DMA((n,)),
            pltpu.SemaphoreType.DMA((n,)),
            pltpu.SemaphoreType.DMA((6,)),
        ],
        compiler_params=pltpu.CompilerParams(
            collective_id=0, has_side_effects=True, vmem_limit_bytes=60 * 1024 * 1024
        ),
    )(
        ctf_class, tile_mask, images.reshape(img_rows, LANES), projections, ctf_table,
        jnp.asarray(phase_rows(BOX)),
    )
    sums = lax.dot_general(
        weights, shifted, (((0,), (0,)), ((), ())), preferred_element_type=jnp.float32
    )
    return ((rescale * sums).astype(jnp.bfloat16), totals[0])


def fits_fused(n, images, projections, ctf_table, tile_mask):
    poses, width = projections.shape
    return (
        images.shape[0] == 1
        and tile_mask.shape == (1, poses // POSE_TILE)
        and n == IMG_TILE
        and poses <= LANES
        and 3 * ctf_table.shape[0] <= LANES
        and width % (4 * CHUNK) == 0
    )


def per_device(images, ctf_class, projections, ctf_table, tile_mask):
    pose_dev = projections.shape[0]
    img_dev = images.shape[0]
    shift_count = len(shift_rows)
    width_total = projections.shape[1]
    cosine_tab, sine_table = phase_tables(BOX)
    norm_table = norm_terms(projections, ctf_table)
    allowed = jnp.repeat(jnp.repeat(tile_mask, IMG_TILE, axis=0), POSE_TILE, axis=1) > 0

    def shifted_block(pixels, classes, block_index, block_rows):
        pix_block = lax.dynamic_slice_in_dim(pixels, block_index * block_rows, block_rows, 0)
        cls_block = lax.dynamic_slice_in_dim(classes, block_index * block_rows, block_rows, 0)
        stacked = make_shifted(pix_block, cls_block, ctf_table, cosine_tab, sine_table)
        return (stacked.reshape(block_rows * shift_count, width_total), cls_block)

    pieces = (
        lax.all_gather(images, "pose", axis=0, tiled=True),
        lax.all_gather(ctf_class, "pose", axis=0, tiled=True),
    )
    pixels = pieces[0]
    classes = pieces[1]
    row_count = pixels.shape[0]
    block_rows = math.gcd(row_count, 32)

    def score_block(block_index):
        stacked, cls_block = shifted_block(pixels, classes, block_index, block_rows)
        raw_scores = jnp.dot(stacked, projections.T, preferred_element_type=jnp.float32)
        raw_scores = raw_scores.reshape(block_rows, shift_count, pose_dev)
        penalty = jnp.dot(
            class_rows(cls_block, ctf_table.shape[0]), norm_table, precision=lax.Precision.HIGHEST
        )
        return raw_scores - 0.5 * penalty[:, None, :]

    blocks = lax.map(score_block, jnp.arange(row_count // block_rows, dtype=jnp.int32))
    scores = blocks.reshape(row_count, shift_count, pose_dev)
    masked = jnp.where(allowed[:, None, :], scores, floor_score)
    local_peak = jnp.max(masked, axis=(1, 2))
    local_total = jnp.sum(
        jnp.where(allowed[:, None, :], jnp.exp(masked - local_peak[:, None, None]), 0.0),
        axis=(1, 2),
    )
    peak, denominator = joined((local_peak, local_total), "pose", combine_stats)
    exponent = jnp.where(allowed[:, None, :], jnp.exp(masked - peak[:, None, None]), 0.0)
    weights = (exponent / denominator[:, None, None]).astype(jnp.bfloat16)
    empty_sums = jnp.zeros((pose_dev, width_total), jnp.float32)
    pieces = (
        lax.all_gather(images, "pose", axis=0, tiled=True),
        lax.all_gather(ctf_class, "pose", axis=0, tiled=True),
    )
    weighted_pixels = pieces[0]
    weighted_classes = pieces[1]
    row_count = weighted_pixels.shape[0]
    weighted_block_rows = math.gcd(row_count, 32)

    def add_block(block_index, partial_sum):
        stacked, cls_block = shifted_block(
            weighted_pixels, weighted_classes, block_index, weighted_block_rows
        )
        weight_block = lax.dynamic_slice_in_dim(
            weights, block_index * weighted_block_rows, weighted_block_rows, 0
        )
        weight_block = weight_block.reshape(weighted_block_rows * shift_count, pose_dev)
        return partial_sum + lax.dot_general(
            weight_block, stacked, (((0,), (0,)), ((), ())), preferred_element_type=jnp.float32
        )

    accumulated = lax.fori_loop(0, row_count // weighted_block_rows, add_block, empty_sums)
    rescale = shift_count * pose_dev / img_dev
    back_sums = (rescale * accumulated).astype(jnp.bfloat16)
    pose_totals = rescale * jnp.sum(weights.astype(jnp.float32), axis=(0, 1))
    return (back_sums, pose_totals)


def solution(mesh):
    in_specs = (
        P(("groups", "pose"), None),
        P(("groups", "pose")),
        P(("groups", "pose"), None),
        P(),
        P("groups", "pose"),
    )
    out_specs = (P(("groups", "pose"), None), P(("groups", "pose")))
    pose_size = mesh.shape["pose"]

    def body(images, ctf_class, projections, ctf_table, tile_mask):
        if fits_fused(pose_size, images, projections, ctf_table, tile_mask):
            return fused(images, ctf_class, projections, ctf_table, tile_mask, pose_size)
        return per_device(images, ctf_class, projections, ctf_table, tile_mask)

    return jax.shard_map(
        body, mesh=mesh, in_specs=in_specs, out_specs=out_specs, check_vma=False
    )
```

```python
import functools
import math

import jax
import jax.numpy as jnp
import numpy as np
from jax import lax
from jax.experimental import pallas as pl
from jax.experimental.pallas import tpu as pltpu
from jax.sharding import PartitionSpec as P

BOX = 192
IMG_TILE = 16
POSE_TILE = 8


shift_rows = (0.0, 1.0, -1.0, 0.0, 0.0)
shift_cols = (0.0, 0.0, 0.0, 1.0, -1.0)
floor_score = -1e30


def joined(value, axis, join):
    pieces = jax.tree.map(lambda part: lax.all_gather(part, axis), value)
    head = jax.tree.map(lambda part: part[0], pieces)
    tail = jax.tree.map(lambda part: part[1:], pieces)
    running, _ = lax.scan(lambda running, slab: (join(running, slab), None), head, tail)
    return running


def phase_tables(box_size):
    half_box = box_size // 2
    coeff_index = jnp.arange(box_size * half_box, dtype=jnp.int32)
    row_index = coeff_index // half_box
    col_index = coeff_index % half_box
    freq_x = jnp.where(row_index < half_box, row_index, row_index - box_size).astype(jnp.float32)
    freq_y = col_index.astype(jnp.float32)
    step_x = jnp.array(shift_rows, jnp.float32)[:, None]
    step_y = jnp.array(shift_cols, jnp.float32)[:, None]
    phases = 2.0 * math.pi / box_size * (step_x * freq_x[None, :] + step_y * freq_y[None, :])
    return (jnp.cos(phases), jnp.sin(phases))


def class_rows(classes, ctf_count):
    return (classes[:, None] == jnp.arange(ctf_count, dtype=jnp.int32)[None, :]).astype(jnp.float32)


def make_shifted(pixels, classes, ctf_table, cosine_tab, sine_table):
    half_len = pixels.shape[1] // 2
    one_hot = class_rows(classes, ctf_table.shape[0])
    factor = jnp.dot(one_hot, ctf_table, precision=lax.Precision.HIGHEST)[:, None, :]
    real_part = pixels[:, :half_len].astype(jnp.float32)[:, None, :]
    imag_part = pixels[:, half_len:].astype(jnp.float32)[:, None, :]
    shifted_re = (real_part * cosine_tab[None] + imag_part * sine_table[None]) * factor
    shifted_im = (imag_part * cosine_tab[None] - real_part * sine_table[None]) * factor
    return jnp.concatenate([shifted_re, shifted_im], axis=2).astype(jnp.bfloat16)


def norm_terms(projections, ctf_table):
    squared = ctf_table * ctf_table
    squared = jnp.concatenate([squared, squared], axis=1)
    proj_f = projections.astype(jnp.float32)
    return jnp.dot(squared, (proj_f * proj_f).T, precision=lax.Precision.HIGHEST)


def combine_stats(earlier, latter):
    highest = jnp.maximum(earlier[0], latter[0])
    return (
        highest,
        earlier[1] * jnp.exp(earlier[0] - highest) + latter[1] * jnp.exp(latter[0] - highest),
    )


LANES = 128
CHUNK = 1024
NT = (((1,), (1,)), ((), ()))


def phase_rows(box_size):
    half_box = box_size // 2
    coeff_index = np.arange(box_size * half_box)
    row_index = coeff_index // half_box
    freq_x = np.where(row_index < half_box, row_index, row_index - box_size)
    freq_y = coeff_index % half_box
    turn = 2.0 * math.pi / box_size
    rows = [np.cos(turn * freq_x), np.sin(turn * freq_x), np.cos(turn * freq_y), np.sin(turn * freq_y)]
    return np.stack(rows + rows).astype(np.float32)


def split_bf16(value, pieces):
    parts = []
    for _ in range(pieces):
        part = value.astype(jnp.bfloat16)
        parts.append(part)
        value = value - part.astype(jnp.float32)
    return jnp.concatenate(parts, axis=0)


def posterior_kernel(
    n, factors, rescale, cls_ref, mask_ref, img_hbm, proj_hbm, ctf_hbm, tab_hbm,
    weights_ref, totals_ref, shifted_hbm,
    slots, imgf, proj, ctf, tab, shifted, stats,
    load_sem, img_sem, send_sem, recv_sem, stat_send, stat_recv, out_sem,
):
    nz, ny, nc = factors
    me = lax.axis_index("pose")
    core = lax.rem(me, nc)
    row = lax.rem(lax.div(me, nc), ny)
    deep = lax.div(me, nc * ny)

    def device(z, y, c):
        return (z * ny + y) * nc + c

    poses, width = proj.shape
    half = width // 2
    quarter = half // 2
    img_rows = width // LANES
    slot_rows = slots.shape[1]
    ctf_count = ctf.shape[0]

    loads = [
        pltpu.make_async_copy(ctf_hbm, ctf, load_sem.at[0]),
        pltpu.make_async_copy(tab_hbm, tab, load_sem.at[1]),
    ]
    for j in range(4):
        cols = pl.ds(((j % 2) * 2 + j // 2) * quarter, quarter)
        loads.append(
            pltpu.make_async_copy(proj_hbm.at[:, cols], proj.at[:, cols], load_sem.at[2 + j])
        )
    own = pltpu.make_async_copy(img_hbm, slots.at[me, pl.ds(0, img_rows)], img_sem)
    own.start()
    for copy in (loads[0], loads[2], loads[3], loads[4], loads[5], loads[1]):
        copy.start()
    barrier = pltpu.get_barrier_semaphore()
    for d in range(1, n):
        pl.semaphore_signal(
            barrier, inc=1, device_id={"pose": lax.rem(me + d, n)},
            device_id_type=pl.DeviceIdType.MESH,
        )
    label = cls_ref[0].astype(jnp.float32)
    slots[me, pl.ds(img_rows, slot_rows - img_rows), :] = jnp.full(
        (slot_rows - img_rows, LANES), label, jnp.float32
    ).astype(jnp.bfloat16)
    own.wait()
    pl.semaphore_wait(barrier, n - 1)

    started = []
    cut = slot_rows // 32 * 16
    pieces = ((0, cut), (cut, slot_rows - cut))

    def image_copy(owner, piece, target, slot):
        part = slots.at[owner, pl.ds(*pieces[piece])]
        return pltpu.make_async_remote_copy(
            src_ref=part, dst_ref=part,
            send_sem=send_sem.at[slot], recv_sem=recv_sem.at[owner, piece],
            device_id={"pose": target}, device_id_type=pl.DeviceIdType.MESH,
        )

    def send(owner, piece, target, *needs):
        copy = image_copy(owner, piece, target, len(started))
        started.append((copy, needs))
        run_if(needs, copy.start)

    def run_if(needs, action):
        if needs:
            pl.when(functools.reduce(jnp.logical_and, needs))(action)
        else:
            action()

    def arrive(owner, piece, *needs):
        run_if(needs, image_copy(owner, piece, me, 0).wait_recv)

    across = device(deep, lax.rem(row + 1, ny), core)
    beside = device(deep, row, lax.rem(core + 1, nc))
    up_ok, down_ok = deep + 1 < nz, deep >= 1
    up = device(jnp.minimum(deep + 1, nz - 1), row, core)
    down = device(jnp.maximum(deep - 1, 0), row, core)
    for piece in range(2):
        send(me, piece, up, up_ok)
        send(me, piece, down, down_ok)
        send(me, piece, across)
    for piece in range(2):
        send(me, piece, beside)

    def line_event(d):
        below, above = deep - d >= 0, deep + d < nz
        low = device(jnp.maximum(deep - d, 0), row, core)
        high = device(jnp.minimum(deep + d, nz - 1), row, core)
        for piece in range(2):
            arrive(low, piece, below)
            if d < nz - 1:
                send(low, piece, up, below, up_ok)
            send(low, piece, across, below)
            arrive(high, piece, above)
            if d < nz - 1:
                send(high, piece, down, above, down_ok)
            send(high, piece, across, above)
        for piece in range(2):
            send(low, piece, beside, below)
            send(high, piece, beside, above)

    def across_event(d):
        other = lax.rem(row + 1, ny)
        if d == 0:
            for piece in range(2):
                arrive(across, piece)
                send(across, piece, beside)
            return
        below, above = deep - d >= 0, deep + d < nz
        low = device(jnp.maximum(deep - d, 0), other, core)
        high = device(jnp.minimum(deep + d, nz - 1), other, core)
        for piece in range(2):
            arrive(low, piece, below)
            send(low, piece, beside, below)
            arrive(high, piece, above)
            send(high, piece, beside, above)

    def norm_step(j, total):
        start = pl.multiple_of(j * CHUNK, CHUNK)
        real = proj[:, pl.ds(start, CHUNK)].astype(jnp.float32)
        imag = proj[:, pl.ds(pl.multiple_of(start + half, CHUNK), CHUNK)].astype(jnp.float32)
        gain = ctf[:, pl.ds(start, CHUNK)]
        power = split_bf16(real * real + imag * imag, 2)
        return total + lax.dot_general(
            split_bf16(gain * gain, 2), power, NT, preferred_element_type=jnp.float32
        )

    steps = half // CHUNK
    events = []
    for d in range(1, nz):
        events += [functools.partial(line_event, d), functools.partial(across_event, d - 1)]
    events.append(functools.partial(across_event, nz - 1))
    for copy in loads[:1] + loads[2:]:
        copy.wait()
    norm = jnp.zeros((2 * ctf_count, 2 * poses), jnp.float32)
    for e in range(len(events) + 1):
        bounds = [steps * k // (len(events) + 1) for k in (e, e + 1)]
        norm = lax.fori_loop(*bounds, norm_step, norm)
        if e < len(events):
            events[e]()
    norm = norm[:ctf_count] + norm[ctf_count:]
    norm = norm[:, :poses] + norm[:, poses:]
    loads[1].wait()
    for y in range(ny):
        for z in range(nz):
            for piece in range(2):
                arrive(device(z, y, lax.rem(core + 1, nc)), piece)

    def widen(i, carry):
        imgf[pl.ds(pl.multiple_of(i * slot_rows, 16), slot_rows), :] = slots[i].astype(jnp.float32)
        return carry

    lax.fori_loop(0, n, widen, 0)
    labels = imgf[pl.ds(img_rows, n, stride=slot_rows), :]
    lanes = lax.broadcasted_iota(jnp.int32, (n, LANES), 1)
    one_hot = (labels == lax.rem(lanes, ctf_count).astype(jnp.float32)).astype(jnp.float32)
    picker = one_hot[:, : 3 * ctf_count].astype(jnp.bfloat16)
    half_rows = half // LANES

    def score_step(j, total):
        start = pl.multiple_of(j * CHUNK, CHUNK)
        for begin in (start, pl.multiple_of(start + half, CHUNK)):
            total = total + lax.dot_general(
                shifted[:, pl.ds(begin, CHUNK)], proj[:, pl.ds(begin, CHUNK)], NT,
                preferred_element_type=jnp.float32,
            )
        return total

    def shift_step(j, total):
        total = score_step(j - 1, total)
        fill_step(j)
        return total

    def fill_step(j):
        start = pl.multiple_of(j * CHUNK, CHUNK)
        later = pl.multiple_of(start + half, CHUNK)
        gain = jnp.dot(
            picker, split_bf16(ctf[:, pl.ds(start, CHUNK)], 3), preferred_element_type=jnp.float32
        )
        for k in range(CHUNK // LANES):
            at = j * (CHUNK // LANES) + k
            cols = slice(k * LANES, (k + 1) * LANES)
            place = pl.ds(pl.multiple_of(start + k * LANES, LANES), LANES)
            place_im = pl.ds(pl.multiple_of(later + k * LANES, LANES), LANES)
            factor = gain[:, cols]
            real = imgf[pl.ds(at, n, stride=slot_rows), :] * factor
            imag = imgf[pl.ds(at + half_rows, n, stride=slot_rows), :] * factor
            shifted[0:n, place] = real.astype(jnp.bfloat16)
            shifted[0:n, place_im] = imag.astype(jnp.bfloat16)
            for axis in range(2):
                cosine = tab[2 * axis : 2 * axis + 1, place]
                sine = tab[2 * axis + 1 : 2 * axis + 2, place]
                first, second = real * cosine, imag * sine
                third, fourth = imag * cosine, real * sine
                low = (2 * axis + 1) * n
                shifted[low : low + n, place] = (first + second).astype(jnp.bfloat16)
                shifted[low : low + n, place_im] = (third - fourth).astype(jnp.bfloat16)
                shifted[low + n : low + 2 * n, place] = (first - second).astype(jnp.bfloat16)
                shifted[low + n : low + 2 * n, place_im] = (third + fourth).astype(jnp.bfloat16)

    shift_count = shifted.shape[0] // n
    raw = jnp.zeros((shift_count * n, poses), jnp.float32)
    written = []
    fill_step(0)
    for part in range(3):
        bounds = [steps * k // 3 for k in (part, part + 1)]
        raw = lax.fori_loop(max(bounds[0], 1), bounds[1], shift_step, raw)
        for base in (0, half):
            cols = pl.ds(base + bounds[0] * CHUNK, (bounds[1] - bounds[0]) * CHUNK)
            copy = pltpu.make_async_copy(
                shifted.at[:, cols], shifted_hbm.at[:, cols], out_sem.at[len(written)]
            )
            copy.start()
            written.append(copy)
    raw = score_step(steps - 1, raw)

    penalty = 0.5 * jnp.dot(
        one_hot[:, :ctf_count], norm,
        precision=lax.Precision.HIGHEST, preferred_element_type=jnp.float32,
    )
    tile = lax.div(lax.broadcasted_iota(jnp.int32, (n, poses), 1), POSE_TILE)
    allowed = jnp.zeros((n, poses), jnp.int32)
    for j in range(poses // POSE_TILE):
        allowed = jnp.where(tile == j, mask_ref[0, j], allowed)
    allowed = allowed > 0
    masked = [
        jnp.where(allowed, raw[t * n : (t + 1) * n] - penalty, floor_score)
        for t in range(shift_count)
    ]
    highest = functools.reduce(jnp.maximum, masked)
    peak = jnp.max(highest, axis=1, keepdims=True)
    mass = sum(jnp.where(allowed, jnp.exp(part - peak), 0.0) for part in masked)
    mass = jnp.sum(mass, axis=1, keepdims=True)
    stats[me, 0:n, :] = jnp.broadcast_to(peak, (n, LANES))
    stats[me, n : 2 * n, :] = jnp.broadcast_to(mass, (n, LANES))

    def stat_copy(owner, target, slot):
        return pltpu.make_async_remote_copy(
            src_ref=stats.at[owner], dst_ref=stats.at[owner],
            send_sem=stat_send.at[slot], recv_sem=stat_recv.at[owner],
            device_id={"pose": target}, device_id_type=pl.DeviceIdType.MESH,
        )

    sent = [stat_copy(me, lax.rem(me + d, n), d - 1) for d in range(1, n)]
    for copy in sent:
        copy.start()
    for d in range(1, n):
        stat_copy(lax.rem(me + d, n), me, d - 1).wait_recv()
    top = functools.reduce(jnp.maximum, [stats[j, 0:n, :] for j in range(n)])
    total = sum(stats[j, n : 2 * n, :] * jnp.exp(stats[j, 0:n, :] - top) for j in range(n))
    top = top[:, :poses]
    total = total[:, :poses]
    column = jnp.zeros((n, poses), jnp.float32)
    for t in range(shift_count):
        weight = jnp.where(allowed, jnp.exp(masked[t] - top), 0.0) / total
        weight = weight.astype(jnp.bfloat16)
        weights_ref[t * n : (t + 1) * n, :] = weight
        column = column + weight.astype(jnp.float32)
    totals_ref[...] = rescale * jnp.sum(column, axis=0, keepdims=True)
    for copy, needs in started:
        run_if(needs, copy.wait_send)
    for copy in sent:
        copy.wait_send()
    for copy in written:
        copy.wait()


def back_kernel(rescale, weights_ref, shifted_ref, sums_ref):
    sums = lax.dot_general(
        weights_ref[...], shifted_ref[...], (((0,), (0,)), ((), ())),
        preferred_element_type=jnp.float32,
    )
    sums_ref[...] = (rescale * sums).astype(jnp.bfloat16)


def fused(images, ctf_class, projections, ctf_table, tile_mask, n):
    poses, width = projections.shape
    shift_count = len(shift_rows)
    ctf_count, half = ctf_table.shape
    img_rows = width // LANES
    slot_rows = img_rows + 16
    rescale = shift_count * poses / images.shape[0]
    rows = shift_count * n
    any_spec = pl.BlockSpec(memory_space=pl.ANY)
    smem = pl.BlockSpec(memory_space=pltpu.SMEM)
    vmem = pl.BlockSpec(memory_space=pltpu.VMEM)
    weights, totals, shifted = pl.pallas_call(
        functools.partial(posterior_kernel, n, (n // 4, 2, 2), rescale),
        out_shape=(
            jax.ShapeDtypeStruct((rows, poses), jnp.bfloat16),
            jax.ShapeDtypeStruct((1, poses), jnp.float32),
            jax.ShapeDtypeStruct((rows, width), jnp.bfloat16),
        ),
        in_specs=[smem, smem, any_spec, any_spec, any_spec, any_spec],
        out_specs=(vmem, vmem, any_spec),
        scratch_shapes=[
            pltpu.VMEM((n, slot_rows, LANES), jnp.bfloat16),
            pltpu.VMEM((n * slot_rows, LANES), jnp.float32),
            pltpu.VMEM((poses, width), jnp.bfloat16),
            pltpu.VMEM((ctf_count, half), jnp.float32),
            pltpu.VMEM((8, half), jnp.float32),
            pltpu.VMEM((rows, width), jnp.bfloat16),
            pltpu.VMEM((n, 2 * n, LANES), jnp.float32),
            pltpu.SemaphoreType.DMA((6,)),
            pltpu.SemaphoreType.DMA,
            pltpu.SemaphoreType.DMA((8 * n,)),
            pltpu.SemaphoreType.DMA((n, 2)),
            pltpu.SemaphoreType.DMA((n,)),
            pltpu.SemaphoreType.DMA((n,)),
            pltpu.SemaphoreType.DMA((6,)),
        ],
        compiler_params=pltpu.CompilerParams(
            collective_id=0, has_side_effects=True, vmem_limit_bytes=60 * 1024 * 1024
        ),
    )(
        ctf_class, tile_mask, images.reshape(img_rows, LANES), projections, ctf_table,
        jnp.asarray(phase_rows(BOX)),
    )
    back_sums = pl.pallas_call(
        functools.partial(back_kernel, rescale),
        out_shape=jax.ShapeDtypeStruct((poses, width), jnp.bfloat16),
        grid=(width // (4 * CHUNK),),
        in_specs=[
            pl.BlockSpec((rows, poses), lambda j: (0, 0)),
            pl.BlockSpec((rows, 4 * CHUNK), lambda j: (0, j)),
        ],
        out_specs=pl.BlockSpec((poses, 4 * CHUNK), lambda j: (0, j)),
        compiler_params=pltpu.CompilerParams(vmem_limit_bytes=32 * 1024 * 1024),
    )(weights, shifted)
    return back_sums, totals[0]


def fits_fused(n, images, projections, ctf_table, tile_mask):
    poses, width = projections.shape
    return (
        images.shape[0] == 1
        and tile_mask.shape == (1, poses // POSE_TILE)
        and n == IMG_TILE
        and poses <= LANES
        and 3 * ctf_table.shape[0] <= LANES
        and width % (4 * CHUNK) == 0
    )


def per_device(images, ctf_class, projections, ctf_table, tile_mask):
    pose_dev = projections.shape[0]
    img_dev = images.shape[0]
    shift_count = len(shift_rows)
    width_total = projections.shape[1]
    cosine_tab, sine_table = phase_tables(BOX)
    norm_table = norm_terms(projections, ctf_table)
    allowed = jnp.repeat(jnp.repeat(tile_mask, IMG_TILE, axis=0), POSE_TILE, axis=1) > 0

    def shifted_block(pixels, classes, block_index, block_rows):
        pix_block = lax.dynamic_slice_in_dim(pixels, block_index * block_rows, block_rows, 0)
        cls_block = lax.dynamic_slice_in_dim(classes, block_index * block_rows, block_rows, 0)
        stacked = make_shifted(pix_block, cls_block, ctf_table, cosine_tab, sine_table)
        return (stacked.reshape(block_rows * shift_count, width_total), cls_block)

    pieces = (
        lax.all_gather(images, "pose", axis=0, tiled=True),
        lax.all_gather(ctf_class, "pose", axis=0, tiled=True),
    )
    pixels = pieces[0]
    classes = pieces[1]
    row_count = pixels.shape[0]
    block_rows = math.gcd(row_count, 32)

    def score_block(block_index):
        stacked, cls_block = shifted_block(pixels, classes, block_index, block_rows)
        raw_scores = jnp.dot(stacked, projections.T, preferred_element_type=jnp.float32)
        raw_scores = raw_scores.reshape(block_rows, shift_count, pose_dev)
        penalty = jnp.dot(
            class_rows(cls_block, ctf_table.shape[0]), norm_table, precision=lax.Precision.HIGHEST
        )
        return raw_scores - 0.5 * penalty[:, None, :]

    blocks = lax.map(score_block, jnp.arange(row_count // block_rows, dtype=jnp.int32))
    scores = blocks.reshape(row_count, shift_count, pose_dev)
    masked = jnp.where(allowed[:, None, :], scores, floor_score)
    local_peak = jnp.max(masked, axis=(1, 2))
    local_total = jnp.sum(
        jnp.where(allowed[:, None, :], jnp.exp(masked - local_peak[:, None, None]), 0.0),
        axis=(1, 2),
    )
    peak, denominator = joined((local_peak, local_total), "pose", combine_stats)
    exponent = jnp.where(allowed[:, None, :], jnp.exp(masked - peak[:, None, None]), 0.0)
    weights = (exponent / denominator[:, None, None]).astype(jnp.bfloat16)
    empty_sums = jnp.zeros((pose_dev, width_total), jnp.float32)
    pieces = (
        lax.all_gather(images, "pose", axis=0, tiled=True),
        lax.all_gather(ctf_class, "pose", axis=0, tiled=True),
    )
    weighted_pixels = pieces[0]
    weighted_classes = pieces[1]
    row_count = weighted_pixels.shape[0]
    weighted_block_rows = math.gcd(row_count, 32)

    def add_block(block_index, partial_sum):
        stacked, cls_block = shifted_block(
            weighted_pixels, weighted_classes, block_index, weighted_block_rows
        )
        weight_block = lax.dynamic_slice_in_dim(
            weights, block_index * weighted_block_rows, weighted_block_rows, 0
        )
        weight_block = weight_block.reshape(weighted_block_rows * shift_count, pose_dev)
        return partial_sum + lax.dot_general(
            weight_block, stacked, (((0,), (0,)), ((), ())), preferred_element_type=jnp.float32
        )

    accumulated = lax.fori_loop(0, row_count // weighted_block_rows, add_block, empty_sums)
    rescale = shift_count * pose_dev / img_dev
    back_sums = (rescale * accumulated).astype(jnp.bfloat16)
    pose_totals = rescale * jnp.sum(weights.astype(jnp.float32), axis=(0, 1))
    return (back_sums, pose_totals)


def solution(mesh):
    in_specs = (
        P(("groups", "pose"), None),
        P(("groups", "pose")),
        P(("groups", "pose"), None),
        P(),
        P("groups", "pose"),
    )
    out_specs = (P(("groups", "pose"), None), P(("groups", "pose")))
    pose_size = mesh.shape["pose"]

    def body(images, ctf_class, projections, ctf_table, tile_mask):
        if fits_fused(pose_size, images, projections, ctf_table, tile_mask):
            return fused(images, ctf_class, projections, ctf_table, tile_mask, pose_size)
        return per_device(images, ctf_class, projections, ctf_table, tile_mask)

    return jax.shard_map(
        body, mesh=mesh, in_specs=in_specs, out_specs=out_specs, check_vma=False
    )
```
